512 devices in a mesh: vocab: 128 (over y, z, core), tok: 4 (over x).
Axes of the slice: x: 4, y: 4, z: 16, core: 2. Of those that a mesh axis runs over, the one named last changes fastest.
Arguments:
- hidden: bfloat16 [512, 16384], P('vocab', 'tok'), may hold values from -5.5 to 5.5
- head: bfloat16 [16384, 65536], P('tok', 'vocab'), may hold values from -1 to 1
- targets: int32 [512], replicated, may hold values from 0 to 65535
- segment_ids: int32 [512], replicated, may hold values from 0 to 7, never falling along the last dimension, each value on 1 to 128 neighbouring positions
- grad_slab: bfloat16 [65536, 64], P('vocab'), may hold values from -6 to 6
- feature_slab: bfloat16 [16384, 64], P('tok'), may hold values from -0.046875 to 0.046875
Outputs:
- sketch: float32 [8, 4096], replicated
The draws below stay inside these ranges and needn't reach their ends.
All inputs are finite; a program needn't handle non-finite values.
Results may differ from the reference program's by a relative error of at most 0.0016.
Values may be sent and summed in bfloat16 or wider, within the bound.
No kernel may reach another device: no remote copies, remote signals or barrier semaphores. Data moves between devices by JAX's collectives and lax.ppermute only.
A program may use at most 64 MiB of HBM per device.

```python
import math
from functools import partial
import jax
import jax.numpy as jnp
import numpy as np
from jax import lax

D = 16384
V = 65536
R = 64
TOKENS = 512
DOCS = 8


def column_spread(base_key, col_index):
    spread = jax.random.uniform(jax.random.fold_in(jax.random.fold_in(base_key, 101), col_index), (), jnp.float32)
    rising = jnp.exp(math.log(10.0) * col_index.astype(jnp.float32) / V)
    return 0.25 * rising * (0.7 + 0.6 * spread)


def column_values(base_key, col_index, salt):
    values = jax.random.normal(jax.random.fold_in(jax.random.fold_in(base_key, salt), col_index), (D,), jnp.float32)
    return jnp.clip(values, -5.0, 5.0)


def head_column(base_key, col_index):
    variance = column_spread(base_key, col_index)
    return column_values(base_key, col_index, 202) * 3.0 * jnp.sqrt(variance / D)


def draw_head(key, part):
    columns = jnp.arange(V, dtype=jnp.int32)
    make_column = partial(head_column, key)
    values = jax.vmap(make_column)(columns)
    return jnp.clip(values, -1.0, 1.0).T.astype(jnp.bfloat16)


def draw_hidden(key, part):
    own_key = jax.random.fold_in(key, 7)
    scale_key, value_key = jax.random.split(own_key)
    row_scale = jnp.exp(jax.random.uniform(scale_key, (TOKENS, 1), jnp.float32, math.log(0.6), math.log(1.2)))
    values = jnp.clip(jax.random.normal(value_key, (TOKENS, D), jnp.float32), -4.5, 4.5) * row_scale
    return jnp.clip(values, -5.5, 5.5).astype(jnp.bfloat16)


def place_ends(result, stream_key, least, high):
    index_at = [jax.random.randint(jax.random.fold_in(stream_key, axis), (), 0, length) for axis, length in enumerate(result.shape)]
    main_axis = result.shape.index(max(result.shape))
    neighbour = index_at[:main_axis] + [(index_at[main_axis] + 1) % result.shape[main_axis]] + index_at[main_axis + 1:]
    return result.at[tuple(index_at)].set(least).at[tuple(neighbour)].set(high)


def block_levels(key, dims, cuts, low, top_value):
    gain = 1.0
    for position, shards_of in cuts:
        heights = jax.random.uniform(jax.random.fold_in(jax.random.fold_in(key, 6), position), (shards_of,), jnp.float32, low / len(cuts), top_value / len(cuts))
        gain = gain * jnp.repeat(jnp.exp(heights), dims[position] // shards_of).reshape((-1,) + (1,) * (len(dims) - 1 - position))
    return gain


def cumulative_ranks(number_of, skew):
    portions = [(1 << 20) // math.isqrt(rank ** skew) + 1 for rank in range(1, number_of + 1)]
    scale = 1 + sum(portions) // (1 << 30)
    return np.cumsum(np.array([max(1, weight // scale) for weight in portions]))


def skewed_ids(key, shape, amount, lean):
    table = cumulative_ranks(amount, lean)
    ticket = jax.random.randint(jax.random.fold_in(key, 1), shape, 0, int(table[amount - 1]))
    grade = jnp.searchsorted(jnp.asarray(table, jnp.int32), ticket, side="right")
    return jax.random.permutation(jax.random.fold_in(key, 2), amount)[grade].astype(jnp.int32)


def profile(number_of, total, limit, skew):
    portions = [(1 << 20) // math.isqrt(rank ** skew) + 1 for rank in range(2, number_of + 1)]
    surplus, given = total - limit - (number_of - 1), [1] * (number_of - 1)
    while surplus > 0:
        free = [i for i in range(number_of - 1) if given[i] < limit]
        pool, budget = sum([portions[i] for i in free]), surplus
        for i in free:
            addition = min(limit - given[i], max(1, budget * portions[i] // pool), surplus)
            given[i] = given[i] + addition
            surplus = surplus - addition
    return np.array([limit] + given)


def uneven_parts(stream_key, amount, total, reach, lean):
    if amount == 2:
        one = jax.random.randint(stream_key, (), max(1, total - reach), min(reach, total - 1) + 1)
        return jnp.stack([one, total - one])
    tallies = jnp.asarray(profile(amount, total, reach, lean), jnp.int32)
    pairs = (amount - 1) // 2
    giver, receiver = tallies[1:1 + 2 * pairs:2], tallies[2:2 + 2 * pairs:2]
    slack = jnp.minimum(giver - 1, reach - receiver)
    moved = jax.random.randint(jax.random.fold_in(stream_key, 1), (pairs,), 0, 1 << 20) % (slack + 1)
    tallies = tallies.at[1:1 + 2 * pairs:2].set(giver - moved).at[2:2 + 2 * pairs:2].set(receiver + moved)
    return tallies[jax.random.permutation(jax.random.fold_in(stream_key, 2), amount)]


def normal_values(stream_key, shape, width, reach, shards=(), kind=jnp.bfloat16):
    factor_of = block_levels(stream_key, shape, shards, -0.22, 0.18) if shards else 1.0
    result = jax.random.normal(stream_key, shape, jnp.float32) * width * factor_of
    return jnp.minimum(jnp.maximum(result, -reach), reach).astype(kind)


def setup_inputs(seed: int = 0) -> dict:
    arg_keys = jax.random.split(jax.random.key(seed), 7)
    hidden = draw_hidden(jax.random.fold_in(arg_keys[6], 71), 0)
    head = draw_head(jax.random.fold_in(arg_keys[6], 71), 0)
    targets = place_ends(skewed_ids(arg_keys[2], (TOKENS,), V, 2), jax.random.fold_in(arg_keys[2], 3), 0, V - 1).astype(jnp.int32)
    segment_ids = jnp.searchsorted(jnp.cumsum(uneven_parts(arg_keys[3], DOCS, TOKENS, TOKENS // 4, 1)), jnp.arange(TOKENS), side="right").astype(jnp.int32)
    grad_slab = normal_values(arg_keys[4], (V, R), 1.0, 6.0, ((0, 128),))
    feature_slab = normal_values(arg_keys[5], (D, R), D ** -0.5, 0.046875, ((0, 4),))
    return {"hidden": hidden, "head": head, "targets": targets, "segment_ids": segment_ids, "grad_slab": grad_slab, "feature_slab": feature_slab}


def reference(hidden, head, targets, segment_ids, grad_slab, feature_slab):
    logits = jnp.dot(hidden, head, preferred_element_type=jnp.float32)
    row_top = lax.optimization_barrier(jnp.max(logits, axis=1, keepdims=True))
    exponent = jnp.exp(logits - row_top)
    row_sum = lax.optimization_barrier(jnp.sum(exponent, axis=1, keepdims=True))
    column = lax.broadcasted_iota(jnp.int32, logits.shape, 1)
    onehot = (column == targets[:, None]).astype(jnp.float32)
    gradient = (exponent / row_sum - onehot).astype(jnp.bfloat16)
    grad_sketch = jnp.dot(gradient, grad_slab, preferred_element_type=jnp.float32)
    feat_sketch = jnp.dot(hidden, feature_slab, preferred_element_type=jnp.float32)
    documents = lax.broadcasted_iota(jnp.int32, (1, DOCS), 1)
    member = (segment_ids[:, None] == documents).astype(jnp.float32)
    counts = lax.optimization_barrier(jnp.sum(member, axis=0))
    outer_rows = (grad_sketch[:, :, None] * feat_sketch[:, None, :]).reshape(TOKENS, R * R)
    summed = jnp.dot(member.T, outer_rows, precision=lax.Precision.HIGHEST)
    return summed / jnp.sqrt(counts)[:, None]
```

```python
import functools

import jax
import jax.numpy as jnp
from jax import lax
from jax.experimental import pallas as pl
from jax.experimental.pallas import tpu as pltpu
from jax.sharding import Mesh
from jax.sharding import PartitionSpec as P

NY, NZ, NC, NX = 4, 16, 2, 4
SKETCH = 64
DOCS = 8
LANES = 128
F32 = jnp.float32
HIGHEST = lax.Precision.HIGHEST


def iota(shape, dim):
    return lax.broadcasted_iota(jnp.int32, shape, dim)


def softmax_kernel(place, targets, slab, own, other, out):
    core, x, first_col = place[0], place[1], place[2]
    mine = own[0, :64] + own[1, :64] + own[2, :64] + own[3, :64]
    theirs = other[0] + other[1] + other[2] + other[3]
    logits = jnp.concatenate(
        [jnp.where(core == 0, mine, theirs), jnp.where(core == 0, theirs, mine)], axis=0
    )
    rows, cols = logits.shape
    lane16 = iota((NZ, LANES), 1)
    row16 = iota((NZ, LANES), 0)
    pieces = []
    for c in range(NC):
        for y in range(NY):
            hit = lane16 == row16 * (NC * NX) + (c * NX + x)
            pieces.append(jnp.sum(jnp.where(hit, targets[y : y + 1, :], 0), axis=1, keepdims=True))
    target = jnp.concatenate(pieces, axis=0)
    is_target = iota((rows, cols), 1) + first_col == target
    top = jnp.max(logits, axis=1, keepdims=True)
    exponent = jnp.exp(logits - top)
    total = jnp.sum(exponent, axis=1, keepdims=True)
    target_logit = jnp.sum(jnp.where(is_target, logits, 0.0), axis=1, keepdims=True)
    rest = jnp.where(is_target, 0.0, exponent)
    high = rest.astype(jnp.bfloat16)
    low = (rest - high.astype(F32)).astype(jnp.bfloat16)
    slab_block = slab[...]
    grad = jnp.dot(high, slab_block, preferred_element_type=F32) + jnp.dot(
        low, slab_block, preferred_element_type=F32
    )
    at_target = jnp.dot(is_target.astype(jnp.bfloat16), slab_block, preferred_element_type=F32)
    both = jnp.concatenate([grad, at_target], axis=1)
    diagonal = iota((rows, LANES), 0) == iota((rows, LANES), 1)

    def as_row(column):
        return jnp.sum(jnp.where(diagonal, column, 0.0), axis=0, keepdims=True)

    feat = own[0, 64:65, :LANES] + own[1, 64:65, :LANES] + own[2, 64:65, :LANES] + own[3, 64:65, :LANES]
    zero = jnp.zeros((1, LANES), F32)
    stats = jnp.concatenate(
        [as_row(top), as_row(total), as_row(target_logit), zero, feat, zero, zero, zero], axis=0
    )
    for c in range(NC):
        for y in range(NY):
            first = (c * NY + y) * NZ
            out[y * NC + c, :NZ, :] = both[first : first + NZ]
            out[y * NC + c, NZ:, :] = stats


def merged(parts, count, core, y):
    stats = [parts[i, NZ:, :] for i in range(count)]
    top = functools.reduce(jnp.maximum, [s[0:1] for s in stats])
    scales = [jnp.exp(s[0:1] - top) for s in stats]
    total = sum(scale * s[1:2] for scale, s in zip(scales, stats))
    target_logit = sum(s[2:3] for s in stats)
    lane = iota((NZ, LANES), 1)
    mine = lane == iota((NZ, LANES), 0) + (core * NY + y) * NZ

    def as_column(row):
        return jnp.sum(jnp.where(mine, row, 0.0), axis=1, keepdims=True)

    left = lane < SKETCH
    both = sum(
        parts[i, :NZ, :] * jnp.where(left, as_column(scales[i]), 1.0) for i in range(count)
    )
    return both, top, total, target_logit, as_column


def merge_kernel(place, parts, out):
    core, y = place[0], place[3]
    both, top, total, target_logit, _ = merged(parts, NY * NC, core, y)
    feat = parts[y * NC + core, NZ + 4 : NZ + 5, :]
    zero = jnp.zeros((1, LANES), F32)
    out[:NZ, :] = both
    out[NZ:, :] = jnp.concatenate(
        [top, total, target_logit, zero, feat, zero, zero, zero], axis=0
    )


def finish_kernel(place, parts, out):
    core, y = place[0], place[3]
    both, top, total, target_logit, as_column = merged(parts, NZ, core, y)
    chance = jnp.exp(target_logit - top) / total
    weight = as_column((chance - 1.0).astype(jnp.bfloat16).astype(F32))
    grad = both / as_column(total) + weight * pltpu.roll(both, SKETCH, 1)
    row = iota((NZ, LANES), 0)
    feat = sum(jnp.where(row == z, parts[z, NZ + 4 : NZ + 5, :], 0.0) for z in range(NZ))
    out[...] = jnp.where(iota((NZ, LANES), 1) < SKETCH, grad, pltpu.roll(feat, SKETCH, 1))


def document_kernel(segments, rows, out):
    tokens, half = rows.shape[0], SKETCH * DOCS // 2
    values = rows[...]
    index = iota((tokens, half), 0)
    y, c, x, z = index // 128, (index // 64) % 2, (index // 16) % 4, index % 16
    token = y * 128 + z * 8 + c * 4 + x
    segment = segments[...]
    doc = iota((1, half), 1) % DOCS
    start = jnp.zeros((1, half), jnp.int32)
    stop = jnp.zeros((1, half), jnp.int32)
    inverse = jnp.zeros((DOCS, LANES), F32)
    below = jnp.zeros((1, 1), jnp.int32)
    for s in range(DOCS):
        here = jnp.sum(
            jnp.sum((segment == s).astype(jnp.int32), axis=1, keepdims=True), axis=0, keepdims=True
        )
        start = jnp.where(doc == s, below, start)
        below = below + here
        stop = jnp.where(doc == s, below, stop)
        inverse = jnp.where(iota((DOCS, LANES), 0) == s, 1.0 / jnp.sqrt(here.astype(F32)), inverse)
    member = (token >= start) & (token < stop)
    lane = iota((tokens, LANES), 1)
    swapped = pltpu.roll(values, SKETCH, 1)
    total = jnp.zeros((half, LANES), F32)
    for odd in range(2):
        pick = (iota((LANES, half), 0) == 2 * (iota((LANES, half), 1) // DOCS) + odd).astype(F32)
        spread = jnp.dot(values, pick, precision=HIGHEST, preferred_element_type=F32)
        spread = jnp.where(member, spread, 0.0)
        feat = jnp.where(lane < SKETCH, 0.0, values) if odd else jnp.where(lane < SKETCH, swapped, 0.0)
        total = total + lax.dot_general(
            spread, feat, (((0,), (0,)), ((), ())), precision=HIGHEST, preferred_element_type=F32
        )
    for pair in range(SKETCH // 2):
        out[:, pair * LANES : (pair + 1) * LANES] = total[pair * DOCS : (pair + 1) * DOCS] * inverse


def call(kernel, shape, *args):
    vmem = pl.BlockSpec(memory_space=pltpu.VMEM)
    smem = pl.BlockSpec(memory_space=pltpu.SMEM)
    return pl.pallas_call(
        kernel,
        out_shape=jax.ShapeDtypeStruct(shape, F32),
        in_specs=[smem if a.ndim == 1 else vmem for a in args],
        out_specs=vmem,
        compiler_params=pltpu.CompilerParams(vmem_limit_bytes=48 * 1024 * 1024),
    )(*args)


def to_all(block, axes, count):
    copies = jnp.broadcast_to(block[None], (count,) + block.shape)
    return lax.all_to_all(copies, axes, 0, 0, tiled=True)


def on_device(hidden, head, targets, segment_ids, grad_slab, feature_slab):
    y, c, x = lax.axis_index("y"), lax.axis_index("c"), lax.axis_index("x")
    z = lax.axis_index("z")
    width = hidden.shape[1]
    cols = head.shape[1]
    place = jnp.stack([c, x, ((y * NZ + z) * NC + c) * cols, y]).astype(jnp.int32)
    column = to_all(hidden, "z", NZ)
    column = column.transpose(1, 0, 2).reshape(NX * NZ, width)
    own = to_all(column, "y", NY).reshape(NY * NX * NZ, width)
    other = lax.ppermute(own, "c", [(0, 1), (1, 0)])
    own_logits = jnp.dot(own, head, preferred_element_type=F32)
    quarter = jnp.dot(hidden, feature_slab, preferred_element_type=F32)
    other_logits = jnp.dot(other, head, preferred_element_type=F32)

    def by_owner(a):
        return a.reshape(NY, NX, NZ, cols).transpose(1, 0, 2, 3).reshape(NX, NY * NZ, cols)

    feat = jnp.pad(quarter[:, None, :], ((0, 0), (0, 7), (0, cols - SKETCH)))
    outgoing = jnp.concatenate([by_owner(own_logits), feat, by_owner(other_logits)], axis=1)
    parts = lax.all_to_all(outgoing, "x", 0, 0, tiled=True)
    chunks = call(
        softmax_kernel,
        (NY * NC, NZ + 8, LANES),
        place,
        targets.reshape(NY, LANES),
        grad_slab,
        parts[:, :72],
        parts[:, 72:],
    )
    chunks = lax.all_to_all(chunks, ("y", "c"), 0, 0, tiled=True)
    merged_chunk = call(merge_kernel, (NZ + 8, LANES), place, chunks)
    rows = call(finish_kernel, (NZ, LANES), place, to_all(merged_chunk, "z", NZ))
    everyone = to_all(rows, ("y", "c", "x"), NY * NC * NX).reshape(-1, LANES)
    return call(
        document_kernel,
        (DOCS, SKETCH * SKETCH),
        segment_ids.reshape(NY, LANES),
        everyone,
    )


def solution(mesh):
    fine = Mesh(mesh.devices.reshape(NY, NZ, NC, NX), ("y", "z", "c", "x"))
    vocab = ("y", "z", "c")
    return jax.shard_map(
        on_device,
        mesh=fine,
        in_specs=(P(vocab, "x"), P("x", vocab), P(), P(), P(vocab, None), P("x", None)),
        out_specs=P(),
        check_vma=False,
    )
```

```python
import functools

import jax
import jax.numpy as jnp
from jax import lax
from jax.experimental import pallas as pl
from jax.experimental.pallas import tpu as pltpu
from jax.sharding import Mesh
from jax.sharding import PartitionSpec as P

NY, NZ, NC, NX = 4, 16, 2, 4
SKETCH = 64
DOCS = 8
LANES = 128
F32 = jnp.float32
HIGHEST = lax.Precision.HIGHEST


def iota(shape, dim):
    return lax.broadcasted_iota(jnp.int32, shape, dim)


def softmax_kernel(place, targets, slab, own, other, out):
    core, x, first_col = place[0], place[1], place[2]
    mine = own[0, :64] + own[1, :64] + own[2, :64] + own[3, :64]
    theirs = other[0] + other[1] + other[2] + other[3]
    logits = jnp.concatenate(
        [jnp.where(core == 0, mine, theirs), jnp.where(core == 0, theirs, mine)], axis=0
    )
    rows, cols = logits.shape
    top = jnp.max(logits, axis=1, keepdims=True)
    exponent = jnp.exp(logits - top)
    total = jnp.sum(exponent, axis=1, keepdims=True)
    lane16 = iota((NZ, LANES), 1)
    row16 = iota((NZ, LANES), 0)
    pieces = []
    for c in range(NC):
        for y in range(NY):
            hit = lane16 == row16 * (NC * NX) + (c * NX + x)
            pieces.append(jnp.sum(jnp.where(hit, targets[y : y + 1, :], 0), axis=1, keepdims=True))
    target = jnp.concatenate(pieces, axis=0)
    is_target = iota((rows, cols), 1) + first_col == target
    target_logit = jnp.sum(jnp.where(is_target, logits, 0.0), axis=1, keepdims=True)
    rest = jnp.where(is_target, 0.0, exponent)
    high = rest.astype(jnp.bfloat16)
    low = (rest - high.astype(F32)).astype(jnp.bfloat16)
    slab_block = slab[...]

    def sketched(a):
        return lax.dot_general(a, slab_block, (((1,), (1,)), ((), ())), preferred_element_type=F32)

    grad = sketched(high) + sketched(low)
    at_target = sketched(is_target.astype(jnp.bfloat16))
    both = jnp.concatenate([grad, at_target], axis=1)
    diagonal = iota((rows, LANES), 0) == iota((rows, LANES), 1)

    def as_row(column):
        return jnp.sum(jnp.where(diagonal, column, 0.0), axis=0, keepdims=True)

    feat = own[0, 64:65, :LANES] + own[1, 64:65, :LANES] + own[2, 64:65, :LANES] + own[3, 64:65, :LANES]
    zero = jnp.zeros((1, LANES), F32)
    stats = jnp.concatenate(
        [as_row(top), as_row(total), as_row(target_logit), zero, feat, zero, zero, zero], axis=0
    )
    for c in range(NC):
        for y in range(NY):
            first = (c * NY + y) * NZ
            out[y * NC + c, :NZ, :] = both[first : first + NZ]
            out[y * NC + c, NZ:, :] = stats


def merged(parts, count, core, y):
    stats = [parts[i, NZ:, :] for i in range(count)]
    top = functools.reduce(jnp.maximum, [s[0:1] for s in stats])
    scales = [jnp.exp(s[0:1] - top) for s in stats]
    total = sum(scale * s[1:2] for scale, s in zip(scales, stats))
    target_logit = sum(s[2:3] for s in stats)
    lane = iota((NZ, LANES), 1)
    mine = lane == iota((NZ, LANES), 0) + (core * NY + y) * NZ

    def as_column(row):
        return jnp.sum(jnp.where(mine, row, 0.0), axis=1, keepdims=True)

    left = lane < SKETCH
    both = sum(
        parts[i, :NZ, :] * jnp.where(left, as_column(scales[i]), 1.0) for i in range(count)
    )
    return both, top, total, target_logit, as_column


def merge_kernel(place, parts, out):
    core, y = place[0], place[3]
    both, top, total, target_logit, _ = merged(parts, NY * NC, core, y)
    feat = parts[y * NC + core, NZ + 4 : NZ + 5, :]
    zero = jnp.zeros((1, LANES), F32)
    out[:NZ, :] = both
    out[NZ:, :] = jnp.concatenate(
        [top, total, target_logit, zero, feat, zero, zero, zero], axis=0
    )


def finish_kernel(place, parts, out):
    core, y = place[0], place[3]
    both, top, total, target_logit, as_column = merged(parts, NZ, core, y)
    chance = jnp.exp(target_logit - top) / total
    weight = as_column((chance - 1.0).astype(jnp.bfloat16).astype(F32))
    grad = both / as_column(total) + weight * pltpu.roll(both, SKETCH, 1)
    row = iota((NZ, LANES), 0)
    feat = sum(jnp.where(row == z, parts[z, NZ + 4 : NZ + 5, :], 0.0) for z in range(NZ))
    out[...] = jnp.where(iota((NZ, LANES), 1) < SKETCH, grad, pltpu.roll(feat, SKETCH, 1))


def halves(a):
    high = a.astype(jnp.bfloat16)
    return high, (a - high.astype(F32)).astype(jnp.bfloat16)


def document_kernel(segments, rows, out):
    tokens, half = rows.shape[0], SKETCH * DOCS // 2
    values = rows[...]
    index = iota((1, tokens), 1)
    y, c, x, z = index // 128, (index // 64) % 2, (index // 16) % 4, index % 16
    token = y * 128 + z * 8 + c * 4 + x
    segment = segments[...]
    doc = iota((half, 1), 0) % DOCS
    start = jnp.zeros((half, 1), jnp.int32)
    stop = jnp.zeros((half, 1), jnp.int32)
    inverse = jnp.zeros((DOCS, LANES), F32)
    below = jnp.zeros((1, 1), jnp.int32)
    for s in range(DOCS):
        here = jnp.sum(
            jnp.sum((segment == s).astype(jnp.int32), axis=1, keepdims=True), axis=0, keepdims=True
        )
        start = jnp.where(doc == s, below, start)
        below = below + here
        stop = jnp.where(doc == s, below, stop)
        inverse = jnp.where(iota((DOCS, LANES), 0) == s, 1.0 / jnp.sqrt(here.astype(F32)), inverse)
    member = (token >= start) & (token < stop)
    left = iota((tokens, LANES), 1) < SKETCH
    swapped = pltpu.roll(values, SKETCH, 1)
    grad = halves(values)
    total = jnp.zeros((half, LANES), F32)
    for odd in range(2):
        pick = iota((half, LANES), 1) == 2 * (iota((half, LANES), 0) // DOCS) + odd
        pick = pick.astype(F32).astype(jnp.bfloat16)
        spread = [
            lax.dot_general(pick, g, (((1,), (1,)), ((), ())), preferred_element_type=F32)
            for g in grad
        ]
        high, low = [jnp.where(member, a, 0.0).astype(jnp.bfloat16) for a in spread]
        feat_high, feat_low = halves(jnp.where(left, 0.0, values) if odd else jnp.where(left, swapped, 0.0))
        for a, b in ((high, feat_high), (high, feat_low), (low, feat_high)):
            total = total + jnp.dot(a, b, preferred_element_type=F32)
    for pair in range(SKETCH // 2):
        out[:, pair * LANES : (pair + 1) * LANES] = total[pair * DOCS : (pair + 1) * DOCS] * inverse


def call(kernel, shape, *args):
    vmem = pl.BlockSpec(memory_space=pltpu.VMEM)
    smem = pl.BlockSpec(memory_space=pltpu.SMEM)
    return pl.pallas_call(
        kernel,
        out_shape=jax.ShapeDtypeStruct(shape, F32),
        in_specs=[smem if a.ndim == 1 else vmem for a in args],
        out_specs=vmem,
        compiler_params=pltpu.CompilerParams(vmem_limit_bytes=48 * 1024 * 1024),
    )(*args)


def to_all(block, axes, count):
    copies = jnp.broadcast_to(block[None], (count,) + block.shape)
    return lax.all_to_all(copies, axes, 0, 0, tiled=True)


def on_device(hidden, head, targets, segment_ids, grad_slab, feature_slab):
    y, c, x = lax.axis_index("y"), lax.axis_index("c"), lax.axis_index("x")
    z = lax.axis_index("z")
    width = hidden.shape[1]
    cols = head.shape[1]
    place = jnp.stack([c, x, ((y * NZ + z) * NC + c) * cols, y]).astype(jnp.int32)
    hidden, place = lax.optimization_barrier((hidden, place))
    column = lax.all_gather(hidden, "z")
    column = column.transpose(1, 0, 2).reshape(NX * NZ, width)
    own = to_all(column, "y", NY).reshape(NY * NX * NZ, width)
    other = lax.ppermute(own, "c", [(0, 1), (1, 0)])
    own_logits = jnp.dot(own, head, preferred_element_type=F32)
    quarter = jnp.dot(hidden, feature_slab, preferred_element_type=F32)
    other_logits = jnp.dot(other, head, preferred_element_type=F32)

    def by_owner(a):
        return a.reshape(NY, NX, NZ, cols).transpose(1, 0, 2, 3).reshape(NX, NY * NZ, cols)

    feat = jnp.pad(quarter[:, None, :], ((0, 0), (0, 7), (0, cols - SKETCH)))
    outgoing = jnp.concatenate([by_owner(own_logits), feat, by_owner(other_logits)], axis=1)
    parts = lax.all_to_all(outgoing, "x", 0, 0, tiled=True)
    chunks = call(
        softmax_kernel,
        (NY * NC, NZ + 8, LANES),
        place,
        targets.reshape(NY, LANES),
        grad_slab.T,
        parts[:, :72],
        parts[:, 72:],
    )
    chunks = lax.all_to_all(chunks, ("y", "c"), 0, 0, tiled=True)
    merged_chunk = call(merge_kernel, (NZ + 8, LANES), place, chunks)
    rows = call(finish_kernel, (NZ, LANES), place, to_all(merged_chunk, "z", NZ))
    everyone = to_all(rows, ("y", "c", "x"), NY * NC * NX).reshape(-1, LANES)
    return call(
        document_kernel,
        (DOCS, SKETCH * SKETCH),
        segment_ids.reshape(NY, LANES),
        everyone,
    )


def solution(mesh):
    fine = Mesh(mesh.devices.reshape(NY, NZ, NC, NX), ("y", "z", "c", "x"))
    vocab = ("y", "z", "c")
    return jax.shard_map(
        on_device,
        mesh=fine,
        in_specs=(P(vocab, "x"), P("x", vocab), P(), P(), P(vocab, None), P("x", None)),
        out_specs=P(),
        check_vma=False,
    )
```

```python
import functools

import jax
import jax.numpy as jnp
from jax import lax
from jax.experimental import pallas as pl
from jax.experimental.pallas import tpu as pltpu
from jax.sharding import Mesh
from jax.sharding import PartitionSpec as P

NY, NZ, NC, NX = 4, 16, 2, 4
SKETCH = 64
DOCS = 8
LANES = 128
F32 = jnp.float32
HIGHEST = lax.Precision.HIGHEST


def iota(shape, dim):
    return lax.broadcasted_iota(jnp.int32, shape, dim)


def softmax_kernel(place, targets, slab, partner_slab, parts, out):
    core, x, first_col, partner_col = place[0], place[1], place[2], place[4]
    rows, cols = NY * NZ, slab.shape[1]
    summed = parts[0, :rows] + parts[1, :rows] + parts[2, :rows] + parts[3, :rows]
    blocks = [(summed[:, :cols], slab, first_col), (summed[:, cols:], partner_slab, partner_col)]
    hit = iota((NZ, LANES), 1) == iota((NZ, LANES), 0) * (NC * NX) + (core * NX + x)
    target = jnp.concatenate(
        [
            jnp.sum(jnp.where(hit, targets[y : y + 1, :], 0), axis=1, keepdims=True)
            for y in range(NY)
        ],
        axis=0,
    )
    top = jnp.maximum(*[jnp.max(logits, axis=1, keepdims=True) for logits, _, _ in blocks])
    total = target_logit = grad = at_target = 0.0
    for logits, slab_ref, first in blocks:
        is_target = iota((rows, cols), 1) + first == target
        exponent = jnp.exp(logits - top)
        total += jnp.sum(exponent, axis=1, keepdims=True)
        target_logit += jnp.sum(jnp.where(is_target, logits, 0.0), axis=1, keepdims=True)
        slab_block = slab_ref[...]

        def sketched(a):
            return lax.dot_general(a, slab_block, (((1,), (1,)), ((), ())), preferred_element_type=F32)

        high, low = halves(jnp.where(is_target, 0.0, exponent))
        grad += sketched(high) + sketched(low)
        at_target += sketched(is_target.astype(jnp.bfloat16))
    both = jnp.concatenate([grad, at_target], axis=1)
    diagonal = iota((rows, LANES), 0) == iota((rows, LANES), 1)

    def as_row(column):
        return jnp.sum(jnp.where(diagonal, column, 0.0), axis=0, keepdims=True)

    feat = sum(parts[i, rows : rows + 1, :LANES] for i in range(NX))
    zero = jnp.zeros((1, LANES), F32)
    stats = jnp.concatenate(
        [as_row(top), as_row(total), as_row(target_logit), zero, feat, zero, zero, zero], axis=0
    )
    for y in range(NY):
        out[y, :NZ, :] = both[y * NZ : (y + 1) * NZ]
        out[y, NZ:, :] = stats


def merged(parts, count, y):
    stats = [parts[i, NZ:, :] for i in range(count)]
    top = functools.reduce(jnp.maximum, [s[0:1] for s in stats])
    scales = [jnp.exp(s[0:1] - top) for s in stats]
    total = sum(scale * s[1:2] for scale, s in zip(scales, stats))
    target_logit = sum(s[2:3] for s in stats)
    lane = iota((NZ, LANES), 1)
    mine = lane == iota((NZ, LANES), 0) + y * NZ

    def as_column(row):
        return jnp.sum(jnp.where(mine, row, 0.0), axis=1, keepdims=True)

    left = lane < SKETCH
    both = sum(
        parts[i, :NZ, :] * jnp.where(left, as_column(scales[i]), 1.0) for i in range(count)
    )
    return both, top, total, target_logit, as_column


def merge_kernel(place, parts, out):
    y = place[3]
    both, top, total, target_logit, _ = merged(parts, NY, y)
    feat = parts[y, NZ + 4 : NZ + 5, :]
    zero = jnp.zeros((1, LANES), F32)
    out[:NZ, :] = both
    out[NZ:, :] = jnp.concatenate(
        [top, total, target_logit, zero, feat, zero, zero, zero], axis=0
    )


def finish_kernel(place, parts, out):
    y = place[3]
    both, top, total, target_logit, as_column = merged(parts, NZ, y)
    chance = jnp.exp(target_logit - top) / jnp.where(total > 0, total, 1.0)
    weight = as_column((chance - 1.0).astype(jnp.bfloat16).astype(F32))
    grad = both / as_column(total) + weight * pltpu.roll(both, SKETCH, 1)
    row = iota((NZ, LANES), 0)
    feat = sum(jnp.where(row == z, parts[z, NZ + 4 : NZ + 5, :], 0.0) for z in range(NZ))
    out[...] = jnp.where(iota((NZ, LANES), 1) < SKETCH, grad, pltpu.roll(feat, SKETCH, 1))


def halves(a):
    high = a.astype(jnp.bfloat16)
    return high, (a - high.astype(F32)).astype(jnp.bfloat16)


def document_kernel(segments, rows, out):
    tokens, half = rows.shape[0], SKETCH * DOCS // 2
    values = rows[...]
    index = iota((1, tokens), 1)
    y, c, x, z = index // 128, (index // 64) % 2, (index // 16) % 4, index % 16
    token = y * 128 + z * 8 + c * 4 + x
    segment = segments[...]
    doc = iota((half, 1), 0) % DOCS
    start = jnp.zeros((half, 1), jnp.int32)
    stop = jnp.zeros((half, 1), jnp.int32)
    inverse = jnp.zeros((DOCS, LANES), F32)
    below = jnp.zeros((1, 1), jnp.int32)
    for s in range(DOCS):
        here = jnp.sum(
            jnp.sum((segment == s).astype(jnp.int32), axis=1, keepdims=True), axis=0, keepdims=True
        )
        start = jnp.where(doc == s, below, start)
        below = below + here
        stop = jnp.where(doc == s, below, stop)
        inverse = jnp.where(iota((DOCS, LANES), 0) == s, 1.0 / jnp.sqrt(here.astype(F32)), inverse)
    member = (token >= start) & (token < stop)
    left = iota((tokens, LANES), 1) < SKETCH
    swapped = pltpu.roll(values, SKETCH, 1)
    grad = halves(values)
    total = jnp.zeros((half, LANES), F32)
    for odd in range(2):
        pick = iota((half, LANES), 1) == 2 * (iota((half, LANES), 0) // DOCS) + odd
        pick = pick.astype(F32).astype(jnp.bfloat16)
        spread = [
            lax.dot_general(pick, g, (((1,), (1,)), ((), ())), preferred_element_type=F32)
            for g in grad
        ]
        high, low = [jnp.where(member, a, 0.0).astype(jnp.bfloat16) for a in spread]
        feat_high, feat_low = halves(jnp.where(left, 0.0, values) if odd else jnp.where(left, swapped, 0.0))
        for a, b in ((high, feat_high), (high, feat_low), (low, feat_high)):
            total = total + jnp.dot(a, b, preferred_element_type=F32)
    for pair in range(SKETCH // 2):
        out[:, pair * LANES : (pair + 1) * LANES] = total[pair * DOCS : (pair + 1) * DOCS] * inverse


def logits_kernel(rows, own, partner, hidden, feature_slab, out, weights, total, staged, sems, out_sems):
    steps = sems.shape[0]
    depth, cols = own.shape[0] // steps, own.shape[1]
    copies = []
    for k in range(steps):
        part = pl.ds(k * depth, depth)
        for side, head in enumerate((own, partner)):
            target = weights.at[part, pl.ds(side * cols, cols)]
            copies.append(pltpu.make_async_copy(head.at[part], target, sems.at[k, side]))
    for copy in copies:
        copy.start()
    block = NY * NZ
    quarter = lax.dot_general(
        hidden[...], feature_slab[...], (((1,), (1,)), ((), ())), preferred_element_type=F32
    )
    feat = jnp.concatenate([quarter, jnp.zeros((NX, LANES - SKETCH), F32)], axis=1)
    for j in range(NX):
        staged[j, block:, :] = jnp.zeros((8, 2 * cols), F32)
        staged[j, block : block + 1, :LANES] = feat[j : j + 1]
    for k in range(steps):
        copies[2 * k].wait()
        copies[2 * k + 1].wait()
        part = pl.ds(k * depth, depth)
        term = jnp.dot(rows[:, part], weights[part, :], preferred_element_type=F32)
        if k == 0:
            total[...] = term
        elif k < steps - 1:
            total[...] += term
    sends = []
    for j in range(NX):
        for y in range(NY):
            first = (y * NX + j) * NZ
            staged[j, y * NZ : (y + 1) * NZ, :] = total[first : first + NZ, :] + term[first : first + NZ]
        sends.append(pltpu.make_async_copy(staged.at[j], out.at[j], out_sems.at[j]))
        sends[j].start()
    for send in sends:
        send.wait()


def call(kernel, shape, *args):
    vmem = pl.BlockSpec(memory_space=pltpu.VMEM)
    smem = pl.BlockSpec(memory_space=pltpu.SMEM)
    return pl.pallas_call(
        kernel,
        out_shape=jax.ShapeDtypeStruct(shape, F32),
        in_specs=[smem if a.ndim == 1 else vmem for a in args],
        out_specs=vmem,
        compiler_params=pltpu.CompilerParams(vmem_limit_bytes=16 * 1024 * 1024),
    )(*args)


def all_logits(rows, own, partner, hidden, feature_slab):
    vmem = pl.BlockSpec(memory_space=pltpu.VMEM)
    far = pl.BlockSpec(memory_space=pltpu.HBM)
    width, cols = own.shape
    shape = (NX, NY * NZ + 8, 2 * cols)
    return pl.pallas_call(
        logits_kernel,
        out_shape=jax.ShapeDtypeStruct(shape, F32),
        in_specs=[vmem, far, far, vmem, vmem],
        out_specs=far,
        scratch_shapes=[
            pltpu.VMEM((width, 2 * cols), own.dtype),
            pltpu.VMEM((rows.shape[0], 2 * cols), F32),
            pltpu.VMEM(shape, F32),
            pltpu.SemaphoreType.DMA((4, 2)),
            pltpu.SemaphoreType.DMA((NX,)),
        ],
        compiler_params=pltpu.CompilerParams(vmem_limit_bytes=32 * 1024 * 1024),
    )(rows, own, partner, hidden, feature_slab)


def to_all(block, axes, count):
    copies = jnp.broadcast_to(block[None], (count,) + block.shape)
    return lax.all_to_all(copies, axes, 0, 0, tiled=True)


def on_device(hidden, head, targets, segment_ids, grad_slab, feature_slab):
    y, c, x = lax.axis_index("y"), lax.axis_index("c"), lax.axis_index("x")
    z = lax.axis_index("z")
    width = hidden.shape[1]
    cols = head.shape[1]
    column_of = (y * NZ + z) * NC
    place = jnp.stack([c, x, (column_of + c) * cols, y, (column_of + 1 - c) * cols]).astype(jnp.int32)
    hidden, place = lax.optimization_barrier((hidden, place))
    swap = [(0, 1), (1, 0)]
    partner_head = lax.ppermute(head, "c", swap)
    partner_slab = lax.ppermute(grad_slab.T, "c", swap)
    column = lax.all_gather(hidden, "z")
    column = column.transpose(1, 0, 2).reshape(NX * NZ, width)
    rows = to_all(column, "y", NY).reshape(NY * NX * NZ, width)

    outgoing = all_logits(rows, head, partner_head, hidden, feature_slab.T)
    parts = lax.all_to_all(outgoing, "x", 0, 0, tiled=True)
    chunks = call(
        softmax_kernel,
        (NY, NZ + 8, LANES),
        place,
        targets.reshape(NY, LANES),
        grad_slab.T,
        partner_slab,
        parts,
    )
    chunks = lax.all_to_all(chunks, "y", 0, 0, tiled=True)
    merged_chunk = call(merge_kernel, (NZ + 8, LANES), place, chunks)
    rows = call(finish_kernel, (NZ, LANES), place, to_all(merged_chunk, "z", NZ))
    everyone = to_all(rows, ("y", "c", "x"), NY * NC * NX).reshape(-1, LANES)
    return call(
        document_kernel,
        (DOCS, SKETCH * SKETCH),
        segment_ids.reshape(NY, LANES),
        everyone,
    )


def solution(mesh):
    fine = Mesh(mesh.devices.reshape(NY, NZ, NC, NX), ("y", "z", "c", "x"))
    vocab = ("y", "z", "c")
    return jax.shard_map(
        on_device,
        mesh=fine,
        in_specs=(P(vocab, "x"), P("x", vocab), P(), P(), P(vocab, None), P("x", None)),
        out_specs=P(),
        check_vma=False,
    )
```

```python
import functools

import jax
import jax.numpy as jnp
from jax import lax
from jax.experimental import pallas as pl
from jax.experimental.pallas import tpu as pltpu
from jax.sharding import Mesh
from jax.sharding import PartitionSpec as P

NY, NZ, NC, NX = 4, 16, 2, 4
SKETCH = 64
DOCS = 8
LANES = 128
F32 = jnp.float32
HIGHEST = lax.Precision.HIGHEST


def iota(shape, dim):
    return lax.broadcasted_iota(jnp.int32, shape, dim)


def softmax_kernel(place, targets, slabs, partner_slabs, parts, out):
    core, x, y, z = place[0], place[1], place[2], place[3]
    cols = slabs.shape[2]
    tiles = cols // LANES
    lane, row = iota((NZ, LANES), 1), iota((NZ, LANES), 0)
    hit = lane == row * (NC * NX) + (core * NX + x)
    target = jnp.sum(jnp.where(hit, targets[pl.ds(y, 1), :], 0), axis=1, keepdims=True)
    blocks = []
    for source in range(NY):
        every = functools.reduce(jnp.add, [parts[source * NX + i, : 2 * tiles * NZ] for i in range(NX)])
        for side in range(NC):
            owner = core if side == 0 else 1 - core
            pieces = [every[(side * tiles + t) * NZ :][:NZ] for t in range(tiles)]
            first = ((source * NZ + z) * NC + owner) * cols
            slab = (partner_slabs if side else slabs)[source]
            blocks.append((jnp.concatenate(pieces, axis=1), slab, first))
    tops = [jnp.max(logits, axis=1, keepdims=True) for logits, _, _ in blocks]
    top = functools.reduce(jnp.maximum, tops)
    total = target_logit = sketches = 0.0
    for logits, slab, first in blocks:
        is_target = iota(logits.shape, 1) + first == target
        exponent = jnp.exp(logits - top)
        total += jnp.sum(exponent, axis=1, keepdims=True)
        target_logit += jnp.sum(jnp.where(is_target, logits, 0.0), axis=1, keepdims=True)
        high, low = halves(jnp.where(is_target, 0.0, exponent))
        stacked = jnp.concatenate([high, low, is_target.astype(F32).astype(jnp.bfloat16)], axis=0)
        sketches += lax.dot_general(
            stacked, slab, (((1,), (1,)), ((), ())), preferred_element_type=F32
        )
    both = jnp.concatenate([sketches[:NZ] + sketches[NZ : 2 * NZ], sketches[2 * NZ :]], axis=1)
    feat = jnp.zeros((8, LANES), F32)
    for i in range(NX):
        feat = feat + parts[y * NX + i, 2 * tiles * NZ :]
    pack(both, (top, total, target_logit), feat, out)


def pack(both, columns, feat, out):
    left = iota((NZ, LANES), 1) < SKETCH
    spot = iota((NZ, LANES), 1) == iota((NZ, LANES), 0) + SKETCH
    lines = []
    for column in columns:
        lines += thirds(jnp.sum(jnp.where(spot, column, 0.0), axis=0, keepdims=True))
    lines += thirds(pltpu.roll(feat, SKETCH, 1)[:1])[:2]
    index = iota((NZ, LANES), 0)
    second = both - both.astype(jnp.bfloat16).astype(F32)
    other = jnp.zeros((NZ, LANES), F32)
    for i, line in enumerate(lines):
        other = jnp.where(index == i, line, other)
    out[:, :LANES] = both.astype(jnp.bfloat16)
    out[:, LANES:] = jnp.where(left, second, other).astype(jnp.bfloat16)


def thirds(a):
    high = a.astype(jnp.bfloat16).astype(F32)
    mid = (a - high).astype(jnp.bfloat16).astype(F32)
    return [high, mid, a - high - mid]


def finish_kernel(parts, out):
    boths = [(parts[z, :, :LANES].astype(F32), parts[z, :, LANES:].astype(F32)) for z in range(NZ)]
    stats = [
        [low[k : k + 1] + low[k + 1 : k + 2] + low[k + 2 : k + 3] for k in (0, 3, 6)] for _, low in boths
    ]
    top = functools.reduce(jnp.maximum, [s[0] for s in stats])
    scales = [jnp.exp(s[0] - top) for s in stats]
    lane, row = iota((NZ, LANES), 1), iota((NZ, LANES), 0)
    left, mine = lane < SKETCH, lane == row + SKETCH

    def as_column(line):
        return jnp.sum(jnp.where(mine, line, 0.0), axis=1, keepdims=True)

    total = as_column(sum(scale * s[1] for scale, s in zip(scales, stats)))
    target_logit = as_column(sum(s[2] for s in stats))
    both = jnp.zeros((NZ, LANES), F32)
    for (high, low), scale in zip(boths, scales):
        both = both + jnp.where(left, (high + low) * as_column(scale), high)
    chance = jnp.exp(target_logit - as_column(top)) / total
    weight = (chance - 1.0).astype(jnp.bfloat16).astype(F32)
    grad = both / total + weight * pltpu.roll(both, SKETCH, 1)
    feat = sum(jnp.where(row == z, low[9:10] + low[10:11], 0.0) for z, (_, low) in enumerate(boths))
    out[...] = jnp.where(left, grad, feat)


def halves(a):
    high = a.astype(jnp.bfloat16)
    return high, (a - high.astype(F32)).astype(jnp.bfloat16)


def document_kernel(segments, rows, out):
    tokens, half = rows.shape[0], SKETCH * DOCS // 2
    values = rows[...]
    index = iota((1, tokens), 1)
    y, c, x, z = index // 128, (index // 64) % 2, (index // 16) % 4, index % 16
    token = y * 128 + z * 8 + c * 4 + x
    segment = segments[...]
    doc = iota((half, 1), 0) % DOCS
    start = jnp.zeros((half, 1), jnp.int32)
    stop = jnp.zeros((half, 1), jnp.int32)
    inverse = jnp.zeros((DOCS, LANES), F32)
    below = jnp.zeros((1, 1), jnp.int32)
    for s in range(DOCS):
        here = jnp.sum(
            jnp.sum((segment == s).astype(jnp.int32), axis=1, keepdims=True), axis=0, keepdims=True
        )
        start = jnp.where(doc == s, below, start)
        below = below + here
        stop = jnp.where(doc == s, below, stop)
        inverse = jnp.where(iota((DOCS, LANES), 0) == s, 1.0 / jnp.sqrt(here.astype(F32)), inverse)
    member = (token >= start) & (token < stop)
    left = iota((tokens, LANES), 1) < SKETCH
    swapped = pltpu.roll(values, SKETCH, 1)
    grad = halves(values)
    total = jnp.zeros((half, LANES), F32)
    for odd in range(2):
        pick = iota((half, LANES), 1) == 2 * (iota((half, LANES), 0) // DOCS) + odd
        pick = pick.astype(F32).astype(jnp.bfloat16)
        spread = [
            lax.dot_general(pick, g, (((1,), (1,)), ((), ())), preferred_element_type=F32)
            for g in grad
        ]
        high, low = [jnp.where(member, a, 0.0).astype(jnp.bfloat16) for a in spread]
        feat_high, feat_low = halves(jnp.where(left, 0.0, values) if odd else jnp.where(left, swapped, 0.0))
        for a, b in ((high, feat_high), (high, feat_low), (low, feat_high)):
            total = total + jnp.dot(a, b, preferred_element_type=F32)
    for pair in range(SKETCH // 2):
        out[:, pair * LANES : (pair + 1) * LANES] = total[pair * DOCS : (pair + 1) * DOCS] * inverse


def logits_kernel(rows, own, partner, hidden, feature_slab, out, weights, total, staged, sems, out_sems):
    steps = sems.shape[0]
    depth, cols = own.shape[0] // steps, own.shape[1]
    copies = []
    for k in range(steps):
        part = pl.ds(k * depth, depth)
        copies.append(pltpu.make_async_copy(partner.at[part], weights.at[part], sems.at[k]))
    for copy in copies:
        copy.start()
    tiles = 2 * cols // LANES
    quarter = lax.dot_general(
        hidden[...], feature_slab[...], (((1,), (1,)), ((), ())), preferred_element_type=F32
    )
    feat = jnp.concatenate([quarter, jnp.zeros((NX, LANES - SKETCH), F32)], axis=1)
    for y in range(NY):
        for j in range(NX):
            staged[y * NX + j, tiles * NZ :, :] = jnp.broadcast_to(feat[j : j + 1], (8, LANES))
    for k in range(steps):
        part = pl.ds(k * depth, depth)
        left = jnp.dot(rows[:, part], own[part, :], preferred_element_type=F32)
        copies[k].wait()
        right = jnp.dot(rows[:, part], weights[part, :], preferred_element_type=F32)
        term = jnp.concatenate([left, right], axis=1)
        if k == 0:
            total[...] = term
        elif k < steps - 1:
            total[...] += term
    sends = []
    for y in range(NY):
        for j in range(NX):
            block = y * NX + j
            piece = total[block * NZ : (block + 1) * NZ, :] + term[block * NZ : (block + 1) * NZ]
            for t in range(tiles):
                staged[block, t * NZ : (t + 1) * NZ, :] = piece[:, t * LANES : (t + 1) * LANES]
        part = pl.ds(y * NX, NX)
        sends.append(pltpu.make_async_copy(staged.at[part], out.at[part], out_sems.at[y]))
        sends[y].start()
    for send in sends:
        send.wait()


def call(kernel, shape, *args, dtype=F32):
    vmem = pl.BlockSpec(memory_space=pltpu.VMEM)
    smem = pl.BlockSpec(memory_space=pltpu.SMEM)
    return pl.pallas_call(
        kernel,
        out_shape=jax.ShapeDtypeStruct(shape, dtype),
        in_specs=[smem if a.ndim == 1 else vmem for a in args],
        out_specs=vmem,
        compiler_params=pltpu.CompilerParams(vmem_limit_bytes=16 * 1024 * 1024),
    )(*args)


def all_logits(rows, own, partner, hidden, feature_slab):
    vmem = pl.BlockSpec(memory_space=pltpu.VMEM)
    far = pl.BlockSpec(memory_space=pltpu.HBM)
    width, cols = own.shape
    shape = (NY * NX, NZ * 2 * cols // LANES + 8, LANES)
    return pl.pallas_call(
        logits_kernel,
        out_shape=jax.ShapeDtypeStruct(shape, F32),
        in_specs=[vmem, vmem, far, vmem, vmem],
        out_specs=far,
        scratch_shapes=[
            pltpu.VMEM((width, cols), own.dtype),
            pltpu.VMEM((rows.shape[0], 2 * cols), F32),
            pltpu.VMEM(shape, F32),
            pltpu.SemaphoreType.DMA((4,)),
            pltpu.SemaphoreType.DMA((NY,)),
        ],
        compiler_params=pltpu.CompilerParams(vmem_limit_bytes=32 * 1024 * 1024),
    )(rows, own, partner, hidden, feature_slab)


def to_all(block, axes, count):
    copies = jnp.broadcast_to(block[None], (count,) + block.shape)
    return lax.all_to_all(copies, axes, 0, 0, tiled=True)


def on_device(hidden, head, targets, segment_ids, grad_slab, feature_slab):
    y, c, x = lax.axis_index("y"), lax.axis_index("c"), lax.axis_index("x")
    z = lax.axis_index("z")
    width = hidden.shape[1]
    place = jnp.stack([c, x, y, z]).astype(jnp.int32)
    hidden, place = lax.optimization_barrier((hidden, place))
    partner_head = lax.ppermute(head, "c", [(0, 1), (1, 0)])
    column = lax.all_gather(hidden, "z")
    column = column.transpose(1, 0, 2).reshape(NX * NZ, width)
    beside = jnp.concatenate([column, grad_slab.T], axis=1)
    rows = to_all(beside, "y", NY)
    slabs = rows[:, :, width:]
    rows = rows.reshape(NY * NX * NZ, -1)
    outgoing = all_logits(rows, head, partner_head, hidden, feature_slab.T)
    slabs, outgoing = lax.optimization_barrier((slabs, outgoing))
    partner_slabs = lax.ppermute(slabs, "c", [(0, 1), (1, 0)])
    parts = lax.all_to_all(outgoing, ("y", "x"), 0, 0, tiled=True)
    chunk = call(
        softmax_kernel,
        (NZ, 2 * LANES),
        place,
        targets.reshape(NY, LANES),
        slabs,
        partner_slabs,
        parts,
        dtype=jnp.bfloat16,
    )
    rows = call(finish_kernel, (NZ, LANES), to_all(chunk, "z", NZ))
    everyone = to_all(rows, ("y", "c", "x"), NY * NC * NX).reshape(-1, LANES)
    return call(
        document_kernel,
        (DOCS, SKETCH * SKETCH),
        segment_ids.reshape(NY, LANES),
        everyone,
    )


def solution(mesh):
    fine = Mesh(mesh.devices.reshape(NY, NZ, NC, NX), ("y", "z", "c", "x"))
    vocab = ("y", "z", "c")
    return jax.shard_map(
        on_device,
        mesh=fine,
        in_specs=(P(vocab, "x"), P("x", vocab), P(), P(), P(vocab, None), P("x", None)),
        out_specs=P(),
        check_vma=False,
    )
```

```python
import functools

import jax
import jax.numpy as jnp
from jax import lax
from jax.experimental import pallas as pl
from jax.experimental.pallas import tpu as pltpu
from jax.sharding import Mesh
from jax.sharding import PartitionSpec as P

NY, NZ, NC, NX = 4, 16, 2, 4
SKETCH = 64
DOCS = 8
LANES = 128
F32 = jnp.float32
HIGHEST = lax.Precision.HIGHEST


def iota(shape, dim):
    return lax.broadcasted_iota(jnp.int32, shape, dim)


def softmax_kernel(place, targets, slabs, partner_slabs, parts, out):
    core, x, y, z = place[0], place[1], place[2], place[3]
    cols = slabs.shape[2]
    tiles = cols // LANES
    lane, row = iota((NZ, LANES), 1), iota((NZ, LANES), 0)
    hit = lane == row * (NC * NX) + (core * NX + x)
    target = jnp.sum(jnp.where(hit, targets[pl.ds(y, 1), :], 0), axis=1, keepdims=True)
    blocks = []
    for source in range(NY):
        every = functools.reduce(jnp.add, [parts[source * NX + i, : 2 * tiles * NZ] for i in range(NX)])
        for side in range(NC):
            owner = core if side == 0 else 1 - core
            pieces = [every[(side * tiles + t) * NZ :][:NZ] for t in range(tiles)]
            first = ((source * NZ + z) * NC + owner) * cols
            slab = (partner_slabs if side else slabs)[source]
            blocks.append((jnp.concatenate(pieces, axis=1), slab, first))
    tops = [jnp.max(logits, axis=1, keepdims=True) for logits, _, _ in blocks]
    top = functools.reduce(jnp.maximum, tops)
    total = target_logit = sketches = 0.0
    for logits, slab, first in blocks:
        is_target = iota(logits.shape, 1) + first == target
        exponent = jnp.exp(logits - top)
        total += jnp.sum(exponent, axis=1, keepdims=True)
        target_logit += jnp.sum(jnp.where(is_target, logits, 0.0), axis=1, keepdims=True)
        high, low = halves(jnp.where(is_target, 0.0, exponent))
        stacked = jnp.concatenate([high, low, is_target.astype(F32).astype(jnp.bfloat16)], axis=0)
        sketches += lax.dot_general(
            stacked, slab, (((1,), (1,)), ((), ())), preferred_element_type=F32
        )
    both = jnp.concatenate([sketches[:NZ] + sketches[NZ : 2 * NZ], sketches[2 * NZ :]], axis=1)
    feat = jnp.zeros((8, LANES), F32)
    for i in range(NX):
        feat = feat + parts[y * NX + i, 2 * tiles * NZ :]
    pack(both, (top, total, target_logit), feat, out)


def pack(both, columns, feat, out):
    left = iota((NZ, LANES), 1) < SKETCH
    spot = iota((NZ, LANES), 1) == iota((NZ, LANES), 0) + SKETCH
    lines = []
    for column in columns:
        lines += thirds(jnp.sum(jnp.where(spot, column, 0.0), axis=0, keepdims=True))
    lines += thirds(pltpu.roll(feat, SKETCH, 1)[:1])[:2]
    index = iota((NZ, LANES), 0)
    second = both - both.astype(jnp.bfloat16).astype(F32)
    other = jnp.zeros((NZ, LANES), F32)
    for i, line in enumerate(lines):
        other = jnp.where(index == i, line, other)
    out[:, :LANES] = both.astype(jnp.bfloat16)
    out[:, LANES:] = jnp.where(left, second, other).astype(jnp.bfloat16)


def thirds(a):
    high = a.astype(jnp.bfloat16).astype(F32)
    mid = (a - high).astype(jnp.bfloat16).astype(F32)
    return [high, mid, a - high - mid]


def finish_kernel(parts, out):
    boths = [(parts[z, :, :LANES].astype(F32), parts[z, :, LANES:].astype(F32)) for z in range(NZ)]
    stats = [
        [low[k : k + 1] + low[k + 1 : k + 2] + low[k + 2 : k + 3] for k in (0, 3, 6)] for _, low in boths
    ]
    top = functools.reduce(jnp.maximum, [s[0] for s in stats])
    scales = [jnp.exp(s[0] - top) for s in stats]
    lane, row = iota((NZ, LANES), 1), iota((NZ, LANES), 0)
    left, mine = lane < SKETCH, lane == row + SKETCH

    def as_column(line):
        return jnp.sum(jnp.where(mine, line, 0.0), axis=1, keepdims=True)

    total = as_column(sum(scale * s[1] for scale, s in zip(scales, stats)))
    target_logit = as_column(sum(s[2] for s in stats))
    both = jnp.zeros((NZ, LANES), F32)
    for (high, low), scale in zip(boths, scales):
        both = both + jnp.where(left, (high + low) * as_column(scale), high)
    chance = jnp.exp(target_logit - as_column(top)) / total
    weight = (chance - 1.0).astype(jnp.bfloat16).astype(F32)
    grad = both / total + weight * pltpu.roll(both, SKETCH, 1)
    feat = sum(jnp.where(row == z, low[9:10] + low[10:11], 0.0) for z, (_, low) in enumerate(boths))
    out[...] = jnp.where(left, grad, feat)


def halves(a):
    high = a.astype(jnp.bfloat16)
    return high, (a - high.astype(F32)).astype(jnp.bfloat16)


def document_kernel(segments, rows, out):
    tokens, half = rows.shape[0], SKETCH * DOCS // 2
    values = rows[...]
    index = iota((1, tokens), 1)
    y, c, x, z = index // 128, (index // 64) % 2, (index // 16) % 4, index % 16
    token = y * 128 + z * 8 + c * 4 + x
    segment = segments[...]
    doc = iota((half, 1), 0) % DOCS
    start = jnp.zeros((half, 1), jnp.int32)
    stop = jnp.zeros((half, 1), jnp.int32)
    inverse = jnp.zeros((DOCS, LANES), F32)
    below = jnp.zeros((1, 1), jnp.int32)
    for s in range(DOCS):
        here = jnp.sum(
            jnp.sum((segment == s).astype(jnp.int32), axis=1, keepdims=True), axis=0, keepdims=True
        )
        start = jnp.where(doc == s, below, start)
        below = below + here
        stop = jnp.where(doc == s, below, stop)
        inverse = jnp.where(iota((DOCS, LANES), 0) == s, 1.0 / jnp.sqrt(here.astype(F32)), inverse)
    member = (token >= start) & (token < stop)
    left = iota((tokens, LANES), 1) < SKETCH
    swapped = pltpu.roll(values, SKETCH, 1)
    grad = halves(values)
    total = jnp.zeros((half, LANES), F32)
    for odd in range(2):
        pick = iota((half, LANES), 1) == 2 * (iota((half, LANES), 0) // DOCS) + odd
        pick = pick.astype(F32).astype(jnp.bfloat16)
        spread = [
            lax.dot_general(pick, g, (((1,), (1,)), ((), ())), preferred_element_type=F32)
            for g in grad
        ]
        high, low = [jnp.where(member, a, 0.0).astype(jnp.bfloat16) for a in spread]
        feat_high, feat_low = halves(jnp.where(left, 0.0, values) if odd else jnp.where(left, swapped, 0.0))
        for a, b in ((high, feat_high), (high, feat_low), (low, feat_high)):
            total = total + jnp.dot(a, b, preferred_element_type=F32)
    for pair in range(SKETCH // 2):
        out[:, pair * LANES : (pair + 1) * LANES] = total[pair * DOCS : (pair + 1) * DOCS] * inverse


def logits_kernel(rows, own, partner, hidden, feature_slab, out, weights, total, staged, sems, out_sems):
    steps = sems.shape[0]
    depth, cols = own.shape[0] // steps, own.shape[1]
    copies = []
    for k in range(steps):
        part = pl.ds(k * depth, depth)
        copies.append(pltpu.make_async_copy(partner.at[part], weights.at[part], sems.at[k]))
    for copy in copies:
        copy.start()
    tiles = 2 * cols // LANES
    quarter = lax.dot_general(
        hidden[...], feature_slab[...], (((1,), (1,)), ((), ())), preferred_element_type=F32
    )
    feat = jnp.concatenate([quarter, jnp.zeros((NX, LANES - SKETCH), F32)], axis=1)
    for y in range(NY):
        for j in range(NX):
            staged[y * NX + j, tiles * NZ :, :] = jnp.broadcast_to(feat[j : j + 1], (8, LANES))
    sends = []
    side_rows = tiles * NZ // 2
    for side, head in enumerate((own, weights)):
        for k in range(steps):
            if side:
                copies[k].wait()
            part = pl.ds(k * depth, depth)
            term = jnp.dot(rows[:, part], head[part, :], preferred_element_type=F32)
            total[...] = total[...] + term if k else term
        for y in range(NY):
            for j in range(NX):
                block = y * NX + j
                piece = total[block * NZ : (block + 1) * NZ, :]
                for t in range(tiles // 2):
                    first = side * side_rows + t * NZ
                    staged[block, first : first + NZ, :] = piece[:, t * LANES : (t + 1) * LANES]
            blocks = pl.ds(y * NX, NX)
            span = pl.ds(side * side_rows, side_rows + 8 * side)
            sends.append(
                pltpu.make_async_copy(staged.at[blocks, span], out.at[blocks, span], out_sems.at[side, y])
            )
            sends[-1].start()
    for send in sends:
        send.wait()


def call(kernel, shape, *args, dtype=F32):
    vmem = pl.BlockSpec(memory_space=pltpu.VMEM)
    smem = pl.BlockSpec(memory_space=pltpu.SMEM)
    return pl.pallas_call(
        kernel,
        out_shape=jax.ShapeDtypeStruct(shape, dtype),
        in_specs=[smem if a.ndim == 1 else vmem for a in args],
        out_specs=vmem,
        compiler_params=pltpu.CompilerParams(vmem_limit_bytes=16 * 1024 * 1024),
    )(*args)


def all_logits(rows, own, partner, hidden, feature_slab):
    vmem = pl.BlockSpec(memory_space=pltpu.VMEM)
    far = pl.BlockSpec(memory_space=pltpu.HBM)
    width, cols = own.shape
    shape = (NY * NX, NZ * 2 * cols // LANES + 8, LANES)
    return pl.pallas_call(
        logits_kernel,
        out_shape=jax.ShapeDtypeStruct(shape, F32),
        in_specs=[vmem, vmem, far, vmem, vmem],
        out_specs=far,
        scratch_shapes=[
            pltpu.VMEM((width, cols), own.dtype),
            pltpu.VMEM((rows.shape[0], cols), F32),
            pltpu.VMEM(shape, F32),
            pltpu.SemaphoreType.DMA((4,)),
            pltpu.SemaphoreType.DMA((2, NY)),
        ],
        compiler_params=pltpu.CompilerParams(vmem_limit_bytes=32 * 1024 * 1024),
    )(rows, own, partner, hidden, feature_slab)


def to_all(block, axes, count):
    copies = jnp.broadcast_to(block[None], (count,) + block.shape)
    return lax.all_to_all(copies, axes, 0, 0, tiled=True)


def on_device(hidden, head, targets, segment_ids, grad_slab, feature_slab):
    y, c, x = lax.axis_index("y"), lax.axis_index("c"), lax.axis_index("x")
    z = lax.axis_index("z")
    width = hidden.shape[1]
    place = jnp.stack([c, x, y, z]).astype(jnp.int32)
    hidden, place = lax.optimization_barrier((hidden, place))
    partner_head = lax.ppermute(head, "c", [(0, 1), (1, 0)])
    column = lax.all_gather(hidden, "z")
    column = column.transpose(1, 0, 2).reshape(NX * NZ, width)
    beside = jnp.concatenate([column, grad_slab.T], axis=1)
    rows = to_all(beside, "y", NY)
    slabs = rows[:, :, width:]
    rows = rows.reshape(NY * NX * NZ, -1)
    outgoing = all_logits(rows, head, partner_head, hidden, feature_slab.T)
    slabs, outgoing = lax.optimization_barrier((slabs, outgoing))
    partner_slabs = lax.ppermute(slabs, "c", [(0, 1), (1, 0)])
    parts = lax.all_to_all(outgoing, ("y", "x"), 0, 0, tiled=True)
    chunk = call(
        softmax_kernel,
        (NZ, 2 * LANES),
        place,
        targets.reshape(NY, LANES),
        slabs,
        partner_slabs,
        parts,
        dtype=jnp.bfloat16,
    )
    rows = call(finish_kernel, (NZ, LANES), to_all(chunk, "z", NZ))
    everyone = to_all(rows, ("y", "c", "x"), NY * NC * NX).reshape(-1, LANES)
    return call(
        document_kernel,
        (DOCS, SKETCH * SKETCH),
        segment_ids.reshape(NY, LANES),
        everyone,
    )


def solution(mesh):
    fine = Mesh(mesh.devices.reshape(NY, NZ, NC, NX), ("y", "z", "c", "x"))
    vocab = ("y", "z", "c")
    return jax.shard_map(
        on_device,
        mesh=fine,
        in_specs=(P(vocab, "x"), P("x", vocab), P(), P(), P(vocab, None), P("x", None)),
        out_specs=P(),
        check_vma=False,
    )
```

```python
import functools

import jax
import jax.numpy as jnp
from jax import lax
from jax.experimental import pallas as pl
from jax.experimental.pallas import tpu as pltpu
from jax.sharding import Mesh
from jax.sharding import PartitionSpec as P

NY, NZ, NC, NX = 4, 16, 2, 4
SKETCH = 64
DOCS = 8
LANES = 128
F32 = jnp.float32
HIGHEST = lax.Precision.HIGHEST


def iota(shape, dim):
    return lax.broadcasted_iota(jnp.int32, shape, dim)


def softmax_kernel(place, targets, slabs, partner_slabs, parts, out):
    core, x, y, z = place[0], place[1], place[2], place[3]
    cols = slabs.shape[2]
    tiles = cols // LANES
    lane, row = iota((NZ, LANES), 1), iota((NZ, LANES), 0)
    hit = lane == row * (NC * NX) + (core * NX + x)
    target = jnp.sum(jnp.where(hit, targets[pl.ds(y, 1), :], 0), axis=1, keepdims=True)
    blocks = []
    for source in range(NY):
        every = functools.reduce(jnp.add, [parts[source * NX + i, : 2 * tiles * NZ] for i in range(NX)])
        for side in range(NC):
            owner = core if side == 0 else 1 - core
            pieces = [every[(side * tiles + t) * NZ :][:NZ] for t in range(tiles)]
            first = ((source * NZ + z) * NC + owner) * cols
            slab = (partner_slabs if side else slabs)[source]
            blocks.append((jnp.concatenate(pieces, axis=1), slab, first))
    tops = [jnp.max(logits, axis=1, keepdims=True) for logits, _, _ in blocks]
    top = functools.reduce(jnp.maximum, tops)
    total = target_logit = sketches = 0.0
    for logits, slab, first in blocks:
        is_target = iota(logits.shape, 1) + first == target
        exponent = jnp.exp(logits - top)
        total += jnp.sum(exponent, axis=1, keepdims=True)
        target_logit += jnp.sum(jnp.where(is_target, logits, 0.0), axis=1, keepdims=True)
        high, low = halves(jnp.where(is_target, 0.0, exponent))
        stacked = jnp.concatenate([high, low, is_target.astype(F32).astype(jnp.bfloat16)], axis=0)
        sketches += lax.dot_general(
            stacked, slab, (((1,), (1,)), ((), ())), preferred_element_type=F32
        )
    both = jnp.concatenate([sketches[:NZ] + sketches[NZ : 2 * NZ], sketches[2 * NZ :]], axis=1)
    feat = jnp.zeros((8, LANES), F32)
    for i in range(NX):
        feat = feat + parts[y * NX + i, 2 * tiles * NZ :]
    pack(both, (top, total, target_logit), feat, out)


def pack(both, columns, feat, out):
    left = iota((NZ, LANES), 1) < SKETCH
    spot = iota((NZ, LANES), 1) == iota((NZ, LANES), 0) + SKETCH
    lines = []
    for column in columns:
        lines += thirds(jnp.sum(jnp.where(spot, column, 0.0), axis=0, keepdims=True))
    lines += thirds(pltpu.roll(feat, SKETCH, 1)[:1])[:2]
    index = iota((NZ, LANES), 0)
    second = both - both.astype(jnp.bfloat16).astype(F32)
    other = jnp.zeros((NZ, LANES), F32)
    for i, line in enumerate(lines):
        other = jnp.where(index == i, line, other)
    out[:, :LANES] = both.astype(jnp.bfloat16)
    out[:, LANES:] = jnp.where(left, second, other).astype(jnp.bfloat16)


def thirds(a):
    high = a.astype(jnp.bfloat16).astype(F32)
    mid = (a - high).astype(jnp.bfloat16).astype(F32)
    return [high, mid, a - high - mid]


def finish_kernel(parts, out):
    boths = [(parts[z, :, :LANES].astype(F32), parts[z, :, LANES:].astype(F32)) for z in range(NZ)]
    stats = [
        [low[k : k + 1] + low[k + 1 : k + 2] + low[k + 2 : k + 3] for k in (0, 3, 6)] for _, low in boths
    ]
    top = functools.reduce(jnp.maximum, [s[0] for s in stats])
    scales = [jnp.exp(s[0] - top) for s in stats]
    lane, row = iota((NZ, LANES), 1), iota((NZ, LANES), 0)
    left, mine = lane < SKETCH, lane == row + SKETCH

    def as_column(line):
        return jnp.sum(jnp.where(mine, line, 0.0), axis=1, keepdims=True)

    total = as_column(sum(scale * s[1] for scale, s in zip(scales, stats)))
    target_logit = as_column(sum(s[2] for s in stats))
    both = jnp.zeros((NZ, LANES), F32)
    for (high, low), scale in zip(boths, scales):
        both = both + jnp.where(left, (high + low) * as_column(scale), high)
    chance = jnp.exp(target_logit - as_column(top)) / total
    weight = (chance - 1.0).astype(jnp.bfloat16).astype(F32)
    grad = both / total + weight * pltpu.roll(both, SKETCH, 1)
    feat = sum(jnp.where(row == z, low[9:10] + low[10:11], 0.0) for z, (_, low) in enumerate(boths))
    out[...] = jnp.where(left, grad, feat)


def halves(a):
    high = a.astype(jnp.bfloat16)
    return high, (a - high.astype(F32)).astype(jnp.bfloat16)


def document_kernel(segments, rows, out):
    tokens, half = rows.shape[0], SKETCH * DOCS // 2
    values = rows[...]
    index = iota((1, tokens), 1)
    y, c, x, z = index // 128, (index // 64) % 2, (index // 16) % 4, index % 16
    token = y * 128 + z * 8 + c * 4 + x
    segment = segments[...]
    doc = iota((half, 1), 0) % DOCS
    start = jnp.zeros((half, 1), jnp.int32)
    stop = jnp.zeros((half, 1), jnp.int32)
    inverse = jnp.zeros((DOCS, LANES), F32)
    below = jnp.zeros((1, 1), jnp.int32)
    for s in range(DOCS):
        here = jnp.sum(
            jnp.sum((segment == s).astype(jnp.int32), axis=1, keepdims=True), axis=0, keepdims=True
        )
        start = jnp.where(doc == s, below, start)
        below = below + here
        stop = jnp.where(doc == s, below, stop)
        inverse = jnp.where(iota((DOCS, LANES), 0) == s, 1.0 / jnp.sqrt(here.astype(F32)), inverse)
    member = (token >= start) & (token < stop)
    left = iota((tokens, LANES), 1) < SKETCH
    swapped = pltpu.roll(values, SKETCH, 1)
    grad = halves(values)
    total = jnp.zeros((half, LANES), F32)
    for odd in range(2):
        pick = iota((half, LANES), 1) == 2 * (iota((half, LANES), 0) // DOCS) + odd
        pick = pick.astype(F32).astype(jnp.bfloat16)
        spread = [
            lax.dot_general(pick, g, (((1,), (1,)), ((), ())), preferred_element_type=F32)
            for g in grad
        ]
        high, low = [jnp.where(member, a, 0.0).astype(jnp.bfloat16) for a in spread]
        feat_high, feat_low = halves(jnp.where(left, 0.0, values) if odd else jnp.where(left, swapped, 0.0))
        for a, b in ((high, feat_high), (high, feat_low), (low, feat_high)):
            total = total + jnp.dot(a, b, preferred_element_type=F32)
    for pair in range(SKETCH // 2):
        out[:, pair * LANES : (pair + 1) * LANES] = total[pair * DOCS : (pair + 1) * DOCS] * inverse


def logits_kernel(rows, own, partner, hidden, feature_slab, out, weights, total, staged, sems, out_sems):
    steps = sems.shape[0]
    depth, cols = own.shape[0] // steps, own.shape[1]
    copies = []
    for k in range(steps):
        part = pl.ds(k * depth, depth)
        copies.append(pltpu.make_async_copy(partner.at[part], weights.at[part], sems.at[k]))
    for copy in copies:
        copy.start()
    tiles = 2 * cols // LANES
    quarter = lax.dot_general(
        hidden[...], feature_slab[...], (((1,), (1,)), ((), ())), preferred_element_type=F32
    )
    feat = jnp.concatenate([quarter, jnp.zeros((NX, LANES - SKETCH), F32)], axis=1)
    for y in range(NY):
        for j in range(NX):
            staged[y * NX + j, tiles * NZ :, :] = jnp.broadcast_to(feat[j : j + 1], (8, LANES))
    sends = []
    side_rows = tiles * NZ // 2
    for side, head in enumerate((own, weights)):
        for k in range(steps):
            if side:
                copies[k].wait()
            part = pl.ds(k * depth, depth)
            term = jnp.dot(rows[:, part], head[part, :], preferred_element_type=F32)
            total[...] = total[...] + term if k else term
        for y in range(NY):
            for j in range(NX):
                block = y * NX + j
                piece = total[block * NZ : (block + 1) * NZ, :]
                for t in range(tiles // 2):
                    first = side * side_rows + t * NZ
                    staged[block, first : first + NZ, :] = piece[:, t * LANES : (t + 1) * LANES]
            blocks = pl.ds(y * NX, NX)
            span = pl.ds(side * side_rows, side_rows + 8 * side)
            sends.append(
                pltpu.make_async_copy(staged.at[blocks, span], out.at[blocks, span], out_sems.at[side, y])
            )
            sends[-1].start()
    for send in sends:
        send.wait()


def call(kernel, shape, *args, dtype=F32):
    vmem = pl.BlockSpec(memory_space=pltpu.VMEM)
    smem = pl.BlockSpec(memory_space=pltpu.SMEM)
    return pl.pallas_call(
        kernel,
        out_shape=jax.ShapeDtypeStruct(shape, dtype),
        in_specs=[smem if a.ndim == 1 else vmem for a in args],
        out_specs=vmem,
        compiler_params=pltpu.CompilerParams(vmem_limit_bytes=16 * 1024 * 1024),
    )(*args)


def all_logits(rows, own, partner, hidden, feature_slab):
    vmem = pl.BlockSpec(memory_space=pltpu.VMEM)
    far = pl.BlockSpec(memory_space=pltpu.HBM)
    width, cols = own.shape
    shape = (NY * NX, NZ * 2 * cols // LANES + 8, LANES)
    return pl.pallas_call(
        logits_kernel,
        out_shape=jax.ShapeDtypeStruct(shape, F32),
        in_specs=[vmem, vmem, far, vmem, vmem],
        out_specs=far,
        scratch_shapes=[
            pltpu.VMEM((width, cols), own.dtype),
            pltpu.VMEM((rows.shape[0], cols), F32),
            pltpu.VMEM(shape, F32),
            pltpu.SemaphoreType.DMA((2,)),
            pltpu.SemaphoreType.DMA((2, NY)),
        ],
        compiler_params=pltpu.CompilerParams(vmem_limit_bytes=32 * 1024 * 1024),
    )(rows, own, partner, hidden, feature_slab)


def to_all(block, axes, count):
    copies = jnp.broadcast_to(block[None], (count,) + block.shape)
    return lax.all_to_all(copies, axes, 0, 0, tiled=True)


def on_device(hidden, head, targets, segment_ids, grad_slab, feature_slab):
    y, c, x = lax.axis_index("y"), lax.axis_index("c"), lax.axis_index("x")
    z = lax.axis_index("z")
    width = hidden.shape[1]
    place = jnp.stack([c, x, y, z]).astype(jnp.int32)
    hidden, place = lax.optimization_barrier((hidden, place))
    partner_head = lax.ppermute(head, "c", [(0, 1), (1, 0)])
    column = lax.all_gather(hidden, "z")
    column = column.transpose(1, 0, 2).reshape(NX * NZ, width)
    beside = jnp.concatenate([column, grad_slab.T], axis=1)
    rows = to_all(beside, "y", NY)
    slabs = rows[:, :, width:]
    rows = rows.reshape(NY * NX * NZ, -1)
    outgoing = all_logits(rows, head, partner_head, hidden, feature_slab.T)
    slabs, outgoing = lax.optimization_barrier((slabs, outgoing))
    partner_slabs = lax.ppermute(slabs, "c", [(0, 1), (1, 0)])
    parts = lax.all_to_all(outgoing, ("y", "x"), 0, 0, tiled=True)
    chunk = call(
        softmax_kernel,
        (NZ, 2 * LANES),
        place,
        targets.reshape(NY, LANES),
        slabs,
        partner_slabs,
        parts,
        dtype=jnp.bfloat16,
    )
    rows = call(finish_kernel, (NZ, LANES), to_all(chunk, "z", NZ))
    everyone = to_all(rows, ("y", "c", "x"), NY * NC * NX).reshape(-1, LANES)
    return call(
        document_kernel,
        (DOCS, SKETCH * SKETCH),
        segment_ids.reshape(NY, LANES),
        everyone,
    )


def solution(mesh):
    fine = Mesh(mesh.devices.reshape(NY, NZ, NC, NX), ("y", "z", "c", "x"))
    vocab = ("y", "z", "c")
    return jax.shard_map(
        on_device,
        mesh=fine,
        in_specs=(P(vocab, "x"), P("x", vocab), P(), P(), P(vocab, None), P("x", None)),
        out_specs=P(),
        check_vma=False,
    )
```
